32 devices in a mesh: lon: 4 (over z), grp: 8 (over y, x, core).
Axes of the slice: x: 2, y: 2, z: 4, core: 2. Of those that a mesh axis runs over, the one named last changes fastest.
Arguments:
- columns: bfloat16 [32768, 512], P(('lon', 'grp')), may hold values from -6 to 6
- cos_zenith: bfloat16 [32768], P(('lon', 'grp')), may hold values from 0.049804688 to 1
- sunlit: int32 [32768], P(('lon', 'grp')), may hold values from 0 to 1, as said below
- span_map: int32 [32768], P(('lon', 'grp')), may hold values from 0 to 1023, as said below
- w_in: bfloat16 [512, 1024], replicated, may hold values from -0.25 to 0.25
- w_mid: bfloat16 [1024, 1024], replicated, may hold values from -0.1875 to 0.1875
- w_out: bfloat16 [1024, 256], replicated, may hold values from -0.1875 to 0.1875
Outputs:
- sw_heating: bfloat16 [32768, 128], P(('lon', 'grp'))
- sw_flux: float32 [32768, 128], P(('lon', 'grp'))
The draws below stay inside these ranges and needn't reach their ends.
Inputs may be any that keep to these rules, and one draw needn't show every extreme that they name: Within each block, span_map is a permutation of 0 to 1023. All 128-slot pieces of span_map in all blocks of one strip hold the same number of sunlit columns; that number for strip l and for strip (l + 2) mod 4 add up to 128; in some strip every column is sunlit.
All inputs are finite; a program needn't handle non-finite values.
Results may differ from the reference program's by a relative error of at most 0.0059.
Values may be sent and summed in bfloat16 or wider, within the bound.
A program may use at most 64 MiB of HBM per device.

```python
import math
import jax
import jax.numpy as jnp
from jax import lax

HID = 1024
COLS_DEV = 1024
FEAT = 512
OUTW = 256
PIECE = 128
TOTAL = 32768
N_LON = 4
N_GRP = 8


def layout(key):
    blocks = N_LON * N_GRP
    piece_len = COLS_DEV // N_GRP
    half_lon = N_LON // 2
    key_list = jax.random.split(key, blocks + 1)
    orders = jax.vmap(lambda subkey: jax.random.permutation(subkey, COLS_DEV))(key_list[1:]).astype(jnp.int32)
    offset = jax.random.randint(key_list[0], (), 0, N_LON)
    strip_index = jnp.arange(blocks, dtype=jnp.int32) // N_GRP
    place_index = (strip_index - offset) % N_LON
    near_count = piece_len * (half_lon - place_index) // half_lon
    far_count = piece_len - piece_len * (N_LON - place_index) // half_lon
    counts = jnp.where(place_index < half_lon, near_count, far_count).astype(jnp.int32)
    return (orders, counts)


def draw_span_map(key, part):
    orders, counts = layout(key)
    return orders.reshape(-1)


def draw_sunlit(key, part):
    orders, counts = layout(key)
    blocks = N_LON * N_GRP
    piece_len = COLS_DEV // N_GRP
    shuffle_key = jax.random.fold_in(key, 5)
    piece_keys = jax.random.split(shuffle_key, blocks * N_GRP)
    piece_perms = jax.vmap(lambda subkey: jax.random.permutation(subkey, piece_len))(piece_keys).astype(jnp.int32)
    piece_perms = piece_perms.reshape(blocks, N_GRP, piece_len)
    lit_flag = (piece_perms < counts[:, None, None]).astype(jnp.int32).reshape(blocks, COLS_DEV)
    placed = jax.vmap(lambda order_row, lit_row: jnp.zeros((COLS_DEV,), jnp.int32).at[order_row].set(lit_row))(orders, lit_flag)
    return placed.reshape(-1)


def shard_levels(own_key, shape, cuts, least, largest):
    level, own = 1.0, jax.random.fold_in(own_key, 6)
    for axis_at, blocks in cuts:
        steps = jnp.exp(jax.random.uniform(jax.random.fold_in(own, axis_at), (blocks,), jnp.float32, least / len(cuts), largest / len(cuts)))
        level = level * jnp.repeat(steps, shape[axis_at] // blocks).reshape([-1 if axis == axis_at else 1 for axis in range(len(shape))])
    return level


def gaussian(own_key, shape, scale, reach, cuts=(), kind=jnp.bfloat16):
    result = jax.random.normal(own_key, shape, jnp.float32) * scale
    if len(cuts) > 0:
        result = shard_levels(own_key, shape, cuts, -0.22, 0.18) * result
    return jnp.clip(result, min=-reach, max=reach).astype(kind)


def setup_inputs(seed: int = 0) -> dict:
    streams_of = jax.random.split(jax.random.key(seed), 8)
    columns = gaussian(streams_of[0], (TOTAL, FEAT), 1.0, 6.0, ((0, 32),))
    cos_zenith = jnp.clip(jnp.exp(math.log(1.0) - 2.9996462 * jax.random.uniform(streams_of[1], (TOTAL,), jnp.float32) ** shard_levels(streams_of[1], (TOTAL,), ((0, 32),), -0.2, 0.2)), 0.049804688, 1.0).astype(jnp.bfloat16)
    sunlit = draw_sunlit(jax.random.fold_in(streams_of[7], 71), 0)
    span_map = draw_span_map(jax.random.fold_in(streams_of[7], 71), 0)
    w_in = gaussian(streams_of[4], (FEAT, HID), FEAT ** -0.5, 0.25)
    w_mid = gaussian(streams_of[5], (HID, HID), HID ** -0.5, 0.1875)
    w_out = gaussian(streams_of[6], (HID, OUTW), HID ** -0.5, 0.1875)
    return {"columns": columns, "cos_zenith": cos_zenith, "sunlit": sunlit, "span_map": span_map, "w_in": w_in, "w_mid": w_mid, "w_out": w_out}


def network(row_block, w_in, w_mid, w_out):
    layer_one = jax.nn.silu(jnp.dot(row_block, w_in, preferred_element_type=jnp.float32)).astype(jnp.bfloat16)
    layer_two = jax.nn.silu(jnp.dot(layer_one, w_mid, preferred_element_type=jnp.float32)).astype(jnp.bfloat16)
    return jnp.dot(layer_two, w_out, preferred_element_type=jnp.float32)


def reference(columns, cos_zenith, sunlit, span_map, w_in, w_mid, w_out):
    blocks = N_LON * N_GRP
    levels = w_out.shape[1] // 2
    block_maps = span_map.reshape(blocks, COLS_DEV)

    def regroup(values_in):
        trailing = values_in.shape[1:]
        blocked = values_in.reshape((blocks, COLS_DEV) + trailing)
        ordered = jax.vmap(lambda block_vals, block_map: block_vals[block_map])(blocked, block_maps)
        ordered = ordered.reshape((N_LON, N_GRP, N_GRP, PIECE) + trailing)
        return jnp.swapaxes(ordered, 1, 2).reshape((TOTAL,) + trailing)

    phys_rows = regroup(columns)
    phys_cos = regroup(cos_zenith)
    phys_sun = regroup(sunlit)
    feature_count = columns.shape[1]
    outputs = lax.map(lambda row_block: network(row_block, w_in, w_mid, w_out),
                      phys_rows.reshape(blocks, COLS_DEV, feature_count)).reshape(TOTAL, 2 * levels)
    insolation = phys_sun.astype(jnp.float32) * phys_cos.astype(jnp.float32)
    phys_heating = (insolation[:, None] * outputs[:, :levels]).astype(jnp.bfloat16)
    sw_flux = insolation[:, None] * jax.nn.softplus(outputs[:, levels:])
    restored = phys_heating.reshape(N_LON, N_GRP, N_GRP, PIECE, levels)
    restored = jnp.swapaxes(restored, 1, 2).reshape(blocks, COLS_DEV, levels)
    placed = jax.vmap(lambda block_vals, block_map: jnp.zeros_like(block_vals).at[block_map].set(block_vals))(restored, block_maps)
    return placed.reshape(TOTAL, levels), sw_flux
```

```python
import functools

import jax
import jax.numpy as jnp
from jax import lax
from jax.experimental import pallas as pl
from jax.experimental.pallas import tpu as pltpu
from jax.sharding import PartitionSpec as P

MESH = pl.DeviceIdType.MESH
LANES = 128
ROWS = 256
WIDE = 256
PARTS = 4


def silu(v):
    half = 0.5 * v
    return half + half * jnp.tanh(half)


def softplus(v):
    return jnp.maximum(v, 0.0) + jnp.log(1.0 + jnp.exp(-jnp.abs(v)))


def down(row):
    return jnp.transpose(jnp.broadcast_to(row, (LANES, LANES)))


def kernel(
    groups,
    columns_hbm, cos_hbm, sun_hbm, map_hbm, w_in_hbm, w_mid_hbm, w_out_hbm,
    heat_hbm, flux_hbm,
    columns, cos, sun, smap, w_in, w_mid, w_out,
    onehot, insol, layer_one, layer_two, heat, flux, leaving,
    load_sem, heat_sem, own_sem, send_sem, recv_sem,
):
    rows = columns.shape[0]
    hidden = w_in.shape[1]
    levels = heat.shape[1]
    piece = rows // groups
    per = groups // PARTS
    part_rows = rows // PARTS
    me = lax.axis_index("grp")
    my_part, my_place = me // per, lax.rem(me, per)

    barrier = pltpu.get_barrier_semaphore()
    for off in range(1, groups):
        pl.semaphore_signal(
            barrier, inc=1, device_id={"grp": lax.rem(me + off, groups)}, device_id_type=MESH
        )

    pairs = (
        (map_hbm, smap), (cos_hbm, cos), (sun_hbm, sun),
        (w_in_hbm, w_in), (columns_hbm, columns), (w_mid_hbm, w_mid), (w_out_hbm, w_out),
    )
    loads = [
        pltpu.make_async_copy(src, dst, load_sem.at[at]) for at, (src, dst) in enumerate(pairs)
    ]
    for load in loads:
        load.start()

    for load in loads[:3]:
        load.wait()
    slots = smap[...].astype(jnp.float32)
    light = sun[...].astype(jnp.float32) * cos[...].astype(jnp.float32)
    lane = lax.broadcasted_iota(jnp.int32, (LANES, LANES), 1).astype(jnp.float32)
    for at in range(rows // LANES):
        here = pl.ds(at * LANES, LANES)
        insol[here, :] = down(light[at : at + 1, :])
        wanted = down(slots[at : at + 1, :])
        for k in range(rows // LANES):
            onehot[here, k * LANES : (k + 1) * LANES] = jnp.where(
                wanted == lane + float(k * LANES), 1.0, 0.0
            ).astype(jnp.bfloat16)

    loads[3].wait()
    loads[4].wait()
    heat_copies = []
    for at in range(rows // ROWS):
        here = pl.ds(at * ROWS, ROWS)
        for n in range(0, hidden, WIDE):
            layer_one[at % 2, :, n : n + WIDE] = silu(
                jnp.dot(columns[here, :], w_in[:, n : n + WIDE], preferred_element_type=jnp.float32)
            ).astype(jnp.bfloat16)
        if at == 0:
            loads[5].wait()
        for n in range(0, hidden, WIDE):
            layer_two[at % 2, :, n : n + WIDE] = silu(
                jnp.dot(layer_one[at % 2], w_mid[:, n : n + WIDE], preferred_element_type=jnp.float32)
            ).astype(jnp.bfloat16)
        if at == 0:
            loads[6].wait()
        out = jnp.dot(layer_two[at % 2], w_out[...], preferred_element_type=jnp.float32)
        heat[here, :] = (insol[here, :] * out[:, :levels]).astype(jnp.bfloat16)
        flux[here, :] = (insol[here, :] * softplus(out[:, levels:])).astype(jnp.bfloat16)
        copy = pltpu.make_async_copy(heat.at[here, :], heat_hbm.at[here, :], heat_sem.at[at])
        copy.start()
        heat_copies.append(copy)

    pl.semaphore_wait(barrier, groups - 1)
    copies = []
    own = None
    arriving = pl.ds(pl.multiple_of(me * piece, piece), piece)
    for k in range(PARTS):
        part = lax.rem(my_part + k + 1, PARTS)
        here = pl.ds(pl.multiple_of(part * part_rows, part_rows), part_rows)
        leaving[here, :] = jnp.dot(
            onehot[here, :], flux[...], preferred_element_type=jnp.float32
        ).astype(jnp.bfloat16)
        for j in range(per):
            to = part * per + lax.rem(my_place + j, per)
            source = leaving.at[pl.ds(pl.multiple_of(to * piece, piece), piece), :]
            if k == PARTS - 1 and j == 0:
                own = pltpu.make_async_copy(source, flux_hbm.at[arriving, :], own_sem)
                own.start()
                continue
            copy = pltpu.make_async_remote_copy(
                src_ref=source,
                dst_ref=flux_hbm.at[arriving, :],
                send_sem=send_sem.at[k * per + j],
                recv_sem=recv_sem.at[k * per + j],
                device_id={"grp": to},
                device_id_type=MESH,
            )
            copy.start()
            copies.append(copy)
    for copy in heat_copies:
        copy.wait()
    own.wait()
    for copy in copies:
        copy.wait_recv()
    for copy in copies:
        copy.wait_send()


def body(columns, cos_zenith, sunlit, span_map, w_in, w_mid, w_out):
    rows, feat = columns.shape
    groups = lax.axis_size("grp")
    hidden, width = w_out.shape
    levels = width // 2
    tiles = rows // LANES
    anywhere = pl.BlockSpec(memory_space=pl.ANY)
    bf16 = jnp.bfloat16
    heating, flux = pl.pallas_call(
        functools.partial(kernel, groups),
        out_shape=(
            jax.ShapeDtypeStruct((rows, levels), bf16),
            jax.ShapeDtypeStruct((rows, levels), bf16),
        ),
        in_specs=[anywhere] * 7,
        out_specs=(anywhere, anywhere),
        scratch_shapes=[
            pltpu.VMEM((rows, feat), bf16),
            pltpu.VMEM((tiles, LANES), bf16),
            pltpu.VMEM((tiles, LANES), jnp.int32),
            pltpu.VMEM((tiles, LANES), jnp.int32),
            pltpu.VMEM((feat, hidden), bf16),
            pltpu.VMEM((hidden, hidden), bf16),
            pltpu.VMEM((hidden, width), bf16),
            pltpu.VMEM((rows, rows), bf16),
            pltpu.VMEM((rows, LANES), jnp.float32),
            pltpu.VMEM((2, ROWS, hidden), bf16),
            pltpu.VMEM((2, ROWS, hidden), bf16),
            pltpu.VMEM((rows, levels), bf16),
            pltpu.VMEM((rows, levels), bf16),
            pltpu.VMEM((rows, levels), bf16),
            pltpu.SemaphoreType.DMA((7,)),
            pltpu.SemaphoreType.DMA((rows // ROWS,)),
            pltpu.SemaphoreType.DMA,
            pltpu.SemaphoreType.DMA((groups,)),
            pltpu.SemaphoreType.DMA((groups,)),
        ],
        compiler_params=pltpu.CompilerParams(
            collective_id=0, has_side_effects=True, vmem_limit_bytes=40 * 1024 * 1024
        ),
        cost_estimate=pl.CostEstimate(
            flops=2 * rows * (feat * hidden + hidden * hidden + hidden * width),
            bytes_accessed=6 * 1024 * 1024,
            transcendentals=2 * rows * hidden,
        ),
    )(
        columns,
        cos_zenith.reshape(tiles, LANES),
        sunlit.reshape(tiles, LANES),
        span_map.reshape(tiles, LANES),
        w_in,
        w_mid,
        w_out,
    )
    return heating, flux.astype(jnp.float32)


def solution(mesh):
    in_specs = (
        P(("lon", "grp"), None),
        P(("lon", "grp")),
        P(("lon", "grp")),
        P(("lon", "grp")),
        P(),
        P(),
        P(),
    )
    out_specs = (P(("lon", "grp"), None), P(("lon", "grp"), None))
    return jax.shard_map(body, mesh=mesh, in_specs=in_specs, out_specs=out_specs, check_vma=False)
```

```python
import functools

import jax
import jax.numpy as jnp
from jax import lax
from jax.experimental import pallas as pl
from jax.experimental.pallas import tpu as pltpu
from jax.sharding import PartitionSpec as P

MESH = pl.DeviceIdType.MESH
LANES = 128
ROWS = 256
WIDE = 256
PARTS = 4


def silu(v):
    half = 0.5 * v
    return half + half * jnp.tanh(half)


def softplus(v):
    return jnp.maximum(v, 0.0) + jnp.log(1.0 + jnp.exp(-jnp.abs(v)))


def down(row):
    return jnp.transpose(jnp.broadcast_to(row, (LANES, LANES)))


def kernel(
    groups,
    columns_hbm, cos_hbm, sun_hbm, map_hbm, w_in_hbm, w_mid_hbm, w_out_hbm,
    heat_ref, flux_ref,
    columns, cos, sun, smap, w_in, w_mid, w_out,
    onehot, back, insol, gathered, layer_one, layer_two, heat, leaving,
    load_sem, own_sem, send_sem, recv_sem,
):
    rows = columns.shape[0]
    hidden = w_in.shape[1]
    levels = heat.shape[1]
    piece = rows // groups
    per = groups // PARTS
    part_rows = rows // PARTS
    me = lax.axis_index("grp")
    my_part, my_place = me // per, lax.rem(me, per)

    barrier = pltpu.get_barrier_semaphore()
    for off in range(1, groups):
        pl.semaphore_signal(
            barrier, inc=1, device_id={"grp": lax.rem(me + off, groups)}, device_id_type=MESH
        )

    pairs = (
        (map_hbm, smap), (cos_hbm, cos), (sun_hbm, sun),
        (w_in_hbm, w_in), (columns_hbm, columns), (w_mid_hbm, w_mid), (w_out_hbm, w_out),
    )
    loads = [
        pltpu.make_async_copy(src, dst, load_sem.at[at]) for at, (src, dst) in enumerate(pairs)
    ]
    for load in loads:
        load.start()

    for load in loads[:3]:
        load.wait()
    slots = smap[...].astype(jnp.float32)
    light = sun[...].astype(jnp.float32) * cos[...].astype(jnp.float32)
    lane = lax.broadcasted_iota(jnp.int32, (LANES, LANES), 1).astype(jnp.float32)
    for at in range(rows // LANES):
        here = pl.ds(at * LANES, LANES)
        wanted = down(slots[at : at + 1, :])
        lit = jnp.zeros((LANES, LANES), jnp.float32)
        for k in range(rows // LANES):
            hit = wanted == lane + float(k * LANES)
            onehot[here, k * LANES : (k + 1) * LANES] = jnp.where(hit, 1.0, 0.0).astype(jnp.bfloat16)
            lit = lit + jnp.where(hit, light[k : k + 1, :], 0.0)
        insol[here, :] = jnp.broadcast_to(jnp.sum(lit, axis=1, keepdims=True), (LANES, LANES))

    loads[3].wait()
    loads[4].wait()
    copies = []
    own = None
    arriving = pl.ds(pl.multiple_of(me * piece, piece), piece)
    for k in range(PARTS):
        part = lax.rem(my_part + k + 1, PARTS)
        here = pl.ds(pl.multiple_of(part * part_rows, part_rows), part_rows)
        gathered[k % 2] = jnp.dot(
            onehot[here, :], columns[...], preferred_element_type=jnp.float32
        ).astype(jnp.bfloat16)
        for n in range(0, hidden, WIDE):
            layer_one[k % 2, :, n : n + WIDE] = silu(
                jnp.dot(gathered[k % 2], w_in[:, n : n + WIDE], preferred_element_type=jnp.float32)
            ).astype(jnp.bfloat16)
        if k == 0:
            loads[5].wait()
        for n in range(0, hidden, WIDE):
            layer_two[k % 2, :, n : n + WIDE] = silu(
                jnp.dot(layer_one[k % 2], w_mid[:, n : n + WIDE], preferred_element_type=jnp.float32)
            ).astype(jnp.bfloat16)
        if k == 0:
            loads[6].wait()
        out = jnp.dot(layer_two[k % 2], w_out[...], preferred_element_type=jnp.float32)
        leaving[here, :] = (insol[here, :] * softplus(out[:, levels:])).astype(jnp.bfloat16)
        heat[here, :] = (insol[here, :] * out[:, :levels]).astype(jnp.bfloat16)
        if k == 0:
            pl.semaphore_wait(barrier, groups - 1)
        for j in range(per):
            to = part * per + lax.rem(my_place + j, per)
            source = leaving.at[pl.ds(pl.multiple_of(to * piece, piece), piece), :]
            if k == PARTS - 1 and j == 0:
                own = pltpu.make_async_copy(source, flux_ref.at[arriving, :], own_sem)
                own.start()
                continue
            copy = pltpu.make_async_remote_copy(
                src_ref=source,
                dst_ref=flux_ref.at[arriving, :],
                send_sem=send_sem.at[k * per + j],
                recv_sem=recv_sem.at[k * per + j],
                device_id={"grp": to},
                device_id_type=MESH,
            )
            copy.start()
            copies.append(copy)
        if k == 0:
            column = lax.broadcasted_iota(jnp.int32, (LANES, LANES), 0).astype(jnp.float32)
            for at in range(rows // LANES):
                for s in range(rows // LANES):
                    back[at * LANES : (at + 1) * LANES, s * LANES : (s + 1) * LANES] = jnp.where(
                        slots[s : s + 1, :] == column + float(at * LANES), 1.0, 0.0
                    ).astype(jnp.bfloat16)
    for at in range(rows // ROWS):
        here = pl.ds(at * ROWS, ROWS)
        heat_ref[here, :] = jnp.dot(
            back[here, :], heat[...], preferred_element_type=jnp.float32
        ).astype(jnp.bfloat16)
    own.wait()
    for copy in copies:
        copy.wait_recv()
    for copy in copies:
        copy.wait_send()


def body(columns, cos_zenith, sunlit, span_map, w_in, w_mid, w_out):
    rows, feat = columns.shape
    groups = lax.axis_size("grp")
    hidden, width = w_out.shape
    levels = width // 2
    tiles = rows // LANES
    anywhere = pl.BlockSpec(memory_space=pl.ANY)
    bf16 = jnp.bfloat16
    heating, flux = pl.pallas_call(
        functools.partial(kernel, groups),
        out_shape=(
            pltpu.VMEM((rows, levels), bf16),
            pltpu.VMEM((rows, levels), bf16),
        ),
        in_specs=[anywhere] * 7,
        out_specs=(pl.BlockSpec(memory_space=pltpu.VMEM),) * 2,
        scratch_shapes=[
            pltpu.VMEM((rows, feat), bf16),
            pltpu.VMEM((tiles, LANES), bf16),
            pltpu.VMEM((tiles, LANES), jnp.int32),
            pltpu.VMEM((tiles, LANES), jnp.int32),
            pltpu.VMEM((feat, hidden), bf16),
            pltpu.VMEM((hidden, hidden), bf16),
            pltpu.VMEM((hidden, width), bf16),
            pltpu.VMEM((rows, rows), bf16),
            pltpu.VMEM((rows, rows), bf16),
            pltpu.VMEM((rows, LANES), jnp.float32),
            pltpu.VMEM((2, rows // PARTS, feat), bf16),
            pltpu.VMEM((2, rows // PARTS, hidden), bf16),
            pltpu.VMEM((2, rows // PARTS, hidden), bf16),
            pltpu.VMEM((rows, levels), bf16),
            pltpu.VMEM((rows, levels), bf16),
            pltpu.SemaphoreType.DMA((7,)),
            pltpu.SemaphoreType.DMA,
            pltpu.SemaphoreType.DMA((groups,)),
            pltpu.SemaphoreType.DMA((groups,)),
        ],
        compiler_params=pltpu.CompilerParams(
            collective_id=0, has_side_effects=True, vmem_limit_bytes=62 * 1024 * 1024
        ),
        cost_estimate=pl.CostEstimate(
            flops=2 * rows * (feat * hidden + hidden * hidden + hidden * width),
            bytes_accessed=6 * 1024 * 1024,
            transcendentals=2 * rows * hidden,
        ),
    )(
        columns,
        cos_zenith.reshape(tiles, LANES),
        sunlit.reshape(tiles, LANES),
        span_map.reshape(tiles, LANES),
        w_in,
        w_mid,
        w_out,
    )
    return heating, flux.astype(jnp.float32)


def solution(mesh):
    in_specs = (
        P(("lon", "grp"), None),
        P(("lon", "grp")),
        P(("lon", "grp")),
        P(("lon", "grp")),
        P(),
        P(),
        P(),
    )
    out_specs = (P(("lon", "grp"), None), P(("lon", "grp"), None))
    return jax.shard_map(body, mesh=mesh, in_specs=in_specs, out_specs=out_specs, check_vma=False)
```

```python
import functools

import jax
import jax.numpy as jnp
from jax import lax
from jax.experimental import pallas as pl
from jax.experimental.pallas import tpu as pltpu
from jax.sharding import PartitionSpec as P

MESH = pl.DeviceIdType.MESH
LANES = 128
ROWS = 256
WIDE = 256
PARTS = 4
FINISH = 4


def silu(v):
    half = 0.5 * v
    return half + half * jnp.tanh(half)


def softplus(v):
    return jnp.maximum(v, 0.0) + jnp.log(1.0 + jnp.exp(-jnp.abs(v)))


def down(row):
    return jnp.transpose(jnp.broadcast_to(row, (LANES, LANES)))


def kernel(
    groups,
    columns_hbm, cos_hbm, sun_hbm, map_hbm, w_in_hbm, w_mid_hbm, w_out_hbm,
    heat_ref, flux_ref,
    columns, cos, sun, smap, w_in, w_mid, w_out,
    onehot, back, insol, gathered, layer_one, layer_two, heat, leaving,
    load_sem, own_sem, send_sem, recv_sem,
):
    rows = columns.shape[0]
    hidden = w_in.shape[1]
    levels = heat.shape[1]
    piece = rows // groups
    per = groups // PARTS
    part_rows = rows // PARTS
    me = lax.axis_index("grp")
    my_part, my_place = me // per, lax.rem(me, per)

    barrier = pltpu.get_barrier_semaphore()
    for off in range(1, groups):
        pl.semaphore_signal(
            barrier, inc=1, device_id={"grp": lax.rem(me + off, groups)}, device_id_type=MESH
        )

    pairs = (
        (map_hbm, smap), (cos_hbm, cos), (sun_hbm, sun),
        (columns_hbm, columns), (w_in_hbm, w_in), (w_mid_hbm, w_mid), (w_out_hbm, w_out),
    )
    loads = [
        pltpu.make_async_copy(src, dst, load_sem.at[at]) for at, (src, dst) in enumerate(pairs)
    ]
    for load in loads:
        load.start()

    for load in loads[:3]:
        load.wait()
    blocks = rows // LANES
    inside = part_rows // LANES
    slots = smap[...].astype(jnp.float32)
    light = sun[...].astype(jnp.float32) * cos[...].astype(jnp.float32)
    lane = lax.broadcasted_iota(jnp.int32, (LANES, LANES), 1).astype(jnp.float32)
    column = lax.broadcasted_iota(jnp.int32, (LANES, LANES), 0).astype(jnp.float32)

    def part_of(k):
        return lax.rem(my_part + k + 1, PARTS)

    def pick(k, at):
        block = part_of(k) * inside + at
        wanted = down(smap[pl.ds(block, 1), :].astype(jnp.float32))
        here = pl.ds(pl.multiple_of(block * LANES, LANES), LANES)
        lit = jnp.zeros((LANES, LANES), jnp.float32)
        for b in range(blocks):
            hit = wanted == lane + float(b * LANES)
            onehot[here, b * LANES : (b + 1) * LANES] = jnp.where(hit, 1.0, 0.0).astype(jnp.bfloat16)
            lit = lit + jnp.where(hit, light[b : b + 1, :], 0.0)
        insol[here, :] = jnp.broadcast_to(jnp.sum(lit, axis=1, keepdims=True), (LANES, LANES))

    def put(at, s):
        back[at * LANES : (at + 1) * LANES, s * LANES : (s + 1) * LANES] = jnp.where(
            slots[s : s + 1, :] == column + float(at * LANES), 1.0, 0.0
        ).astype(jnp.bfloat16)

    for at in range(inside):
        pick(0, at)
    loads[3].wait()
    copies = []
    own = None
    arriving = pl.ds(pl.multiple_of(me * piece, piece), piece)
    for k in range(PARTS):
        part = part_of(k)
        here = pl.ds(pl.multiple_of(part * part_rows, part_rows), part_rows)
        gathered[k % 2] = jnp.dot(
            onehot[here, :], columns[...], preferred_element_type=jnp.float32
        ).astype(jnp.bfloat16)
        jobs = [
            functools.partial(put, at, s)
            for at in range(k * inside, (k + 1) * inside)
            for s in range(blocks)
        ]
        if k + 1 < PARTS:
            jobs += [functools.partial(pick, k + 1, at) for at in range(inside)]
        tiles = hidden // WIDE
        share = -(-len(jobs) // (2 * tiles))
        if k == 0:
            loads[4].wait()
        for n in range(0, hidden, WIDE):
            layer_one[k % 2, :, n : n + WIDE] = silu(
                jnp.dot(gathered[k % 2], w_in[:, n : n + WIDE], preferred_element_type=jnp.float32)
            ).astype(jnp.bfloat16)
            for job in jobs[:share]:
                job()
            jobs = jobs[share:]
        if k == 0:
            loads[5].wait()
        for n in range(0, hidden, WIDE):
            layer_two[k % 2, :, n : n + WIDE] = silu(
                jnp.dot(layer_one[k % 2], w_mid[:, n : n + WIDE], preferred_element_type=jnp.float32)
            ).astype(jnp.bfloat16)
            for job in jobs[:share]:
                job()
            jobs = jobs[share:]
        if k == 0:
            loads[6].wait()
        out = jnp.dot(layer_two[k % 2], w_out[...], preferred_element_type=jnp.float32)
        leaving[here, :] = (insol[here, :] * softplus(out[:, levels:])).astype(jnp.bfloat16)
        heat[here, :] = (insol[here, :] * out[:, :levels]).astype(jnp.bfloat16)
        if k == 0:
            pl.semaphore_wait(barrier, groups - 1)
        for j in range(per):
            to = part * per + lax.rem(my_place + j, per)
            source = leaving.at[pl.ds(pl.multiple_of(to * piece, piece), piece), :]
            if k == PARTS - 1 and j == 0:
                own = pltpu.make_async_copy(source, flux_ref.at[arriving, :], own_sem)
                own.start()
                continue
            copy = pltpu.make_async_remote_copy(
                src_ref=source,
                dst_ref=flux_ref.at[arriving, :],
                send_sem=send_sem.at[k * per + j],
                recv_sem=recv_sem.at[k * per + j],
                device_id={"grp": to},
                device_id_type=MESH,
            )
            copy.start()
            copies.append(copy)
    for at in range(rows // ROWS):
        here = pl.ds(at * ROWS, ROWS)
        heat_ref[here, :] = jnp.dot(
            back[here, :], heat[...], preferred_element_type=jnp.float32
        ).astype(jnp.bfloat16)
    own.wait()
    for copy in copies:
        copy.wait_recv()
    for copy in copies:
        copy.wait_send()


def finish(heat, flux, heat_hbm, flux_hbm, wide, sem):
    copies = [pltpu.make_async_copy(heat, heat_hbm, sem.at[FINISH])]
    copies[0].start()
    step = flux.shape[0] // FINISH
    for at in range(FINISH):
        here = pl.ds(at * step, step)
        wide[here, :] = flux[here, :].astype(jnp.float32)
        copy = pltpu.make_async_copy(wide.at[here, :], flux_hbm.at[here, :], sem.at[at])
        copy.start()
        copies.append(copy)
    for copy in copies:
        copy.wait()


def body(columns, cos_zenith, sunlit, span_map, w_in, w_mid, w_out):
    rows, feat = columns.shape
    groups = lax.axis_size("grp")
    hidden, width = w_out.shape
    levels = width // 2
    tiles = rows // LANES
    anywhere = pl.BlockSpec(memory_space=pl.ANY)
    bf16 = jnp.bfloat16
    heating, flux = pl.pallas_call(
        functools.partial(kernel, groups),
        out_shape=(
            pltpu.VMEM((rows, levels), bf16),
            pltpu.VMEM((rows, levels), bf16),
        ),
        in_specs=[anywhere] * 7,
        out_specs=(pl.BlockSpec(memory_space=pltpu.VMEM),) * 2,
        scratch_shapes=[
            pltpu.VMEM((rows, feat), bf16),
            pltpu.VMEM((tiles, LANES), bf16),
            pltpu.VMEM((tiles, LANES), jnp.int32),
            pltpu.VMEM((tiles, LANES), jnp.int32),
            pltpu.VMEM((feat, hidden), bf16),
            pltpu.VMEM((hidden, hidden), bf16),
            pltpu.VMEM((hidden, width), bf16),
            pltpu.VMEM((rows, rows), bf16),
            pltpu.VMEM((rows, rows), bf16),
            pltpu.VMEM((rows, LANES), jnp.float32),
            pltpu.VMEM((2, rows // PARTS, feat), bf16),
            pltpu.VMEM((2, rows // PARTS, hidden), bf16),
            pltpu.VMEM((2, rows // PARTS, hidden), bf16),
            pltpu.VMEM((rows, levels), bf16),
            pltpu.VMEM((rows, levels), bf16),
            pltpu.SemaphoreType.DMA((7,)),
            pltpu.SemaphoreType.DMA,
            pltpu.SemaphoreType.DMA((groups,)),
            pltpu.SemaphoreType.DMA((groups,)),
        ],
        compiler_params=pltpu.CompilerParams(
            collective_id=0, has_side_effects=True, vmem_limit_bytes=62 * 1024 * 1024
        ),
        cost_estimate=pl.CostEstimate(
            flops=2 * rows * (feat * hidden + hidden * hidden + hidden * width),
            bytes_accessed=6 * 1024 * 1024,
            transcendentals=2 * rows * hidden,
        ),
    )(
        columns,
        cos_zenith.reshape(tiles, LANES),
        sunlit.reshape(tiles, LANES),
        span_map.reshape(tiles, LANES),
        w_in,
        w_mid,
        w_out,
    )
    return pl.pallas_call(
        finish,
        out_shape=(
            jax.ShapeDtypeStruct((rows, levels), bf16),
            jax.ShapeDtypeStruct((rows, levels), jnp.float32),
        ),
        in_specs=[pl.BlockSpec(memory_space=pltpu.VMEM)] * 2,
        out_specs=(anywhere, anywhere),
        scratch_shapes=[
            pltpu.VMEM((rows, levels), jnp.float32),
            pltpu.SemaphoreType.DMA((FINISH + 1,)),
        ],
        compiler_params=pltpu.CompilerParams(vmem_limit_bytes=4 * 1024 * 1024),
    )(heating, flux)


def solution(mesh):
    in_specs = (
        P(("lon", "grp"), None),
        P(("lon", "grp")),
        P(("lon", "grp")),
        P(("lon", "grp")),
        P(),
        P(),
        P(),
    )
    out_specs = (P(("lon", "grp"), None), P(("lon", "grp"), None))
    return jax.shard_map(body, mesh=mesh, in_specs=in_specs, out_specs=out_specs, check_vma=False)
```

```python
import functools

import jax
import jax.numpy as jnp
from jax import lax
from jax.experimental import pallas as pl
from jax.experimental.pallas import tpu as pltpu
from jax.sharding import PartitionSpec as P

MESH = pl.DeviceIdType.MESH
LANES = 128
ROWS = 256
WIDE = 256
PARTS = 4
FINISH = 4


def silu(v):
    half = 0.5 * v
    return half + half * jnp.tanh(half)


def softplus(v):
    return jnp.maximum(v, 0.0) + jnp.log(1.0 + jnp.exp(-jnp.abs(v)))


def down(row):
    return jnp.transpose(jnp.broadcast_to(row, (LANES, LANES)))


def kernel(
    groups,
    columns_hbm, cos_hbm, sun_hbm, map_hbm, w_in_hbm, w_mid_hbm, w_out_hbm,
    heat_ref, flux_ref,
    columns, cos, sun, smap, w_in, w_mid, w_out,
    onehot, back, insol, gathered, layer_one, layer_two, heat, leaving,
    load_sem, own_sem, send_sem, recv_sem,
):
    rows = columns.shape[0]
    hidden = w_in.shape[1]
    levels = heat.shape[1]
    piece = rows // groups
    per = groups // PARTS
    part_rows = rows // PARTS
    me = lax.axis_index("grp")
    my_part, my_place = me // per, lax.rem(me, per)

    barrier = pltpu.get_barrier_semaphore()
    for off in range(1, groups):
        pl.semaphore_signal(
            barrier, inc=1, device_id={"grp": lax.rem(me + off, groups)}, device_id_type=MESH
        )

    pairs = (
        (map_hbm, smap), (cos_hbm, cos), (sun_hbm, sun),
        (columns_hbm, columns), (w_in_hbm, w_in), (w_mid_hbm, w_mid), (w_out_hbm, w_out),
    )
    loads = [
        pltpu.make_async_copy(src, dst, load_sem.at[at]) for at, (src, dst) in enumerate(pairs)
    ]
    for load in loads:
        load.start()

    for load in loads[:3]:
        load.wait()
    blocks = rows // LANES
    inside = part_rows // LANES
    slots = smap[...].astype(jnp.float32)
    light = sun[...].astype(jnp.float32) * cos[...].astype(jnp.float32)
    lane = lax.broadcasted_iota(jnp.int32, (LANES, LANES), 1).astype(jnp.float32)
    column = lax.broadcasted_iota(jnp.int32, (LANES, LANES), 0).astype(jnp.float32)

    def part_of(k):
        return lax.rem(my_part + k + 1, PARTS)

    def pick(k, at):
        block = part_of(k) * inside + at
        wanted = down(smap[pl.ds(block, 1), :].astype(jnp.float32))
        here = pl.ds(pl.multiple_of(block * LANES, LANES), LANES)
        lit = jnp.zeros((LANES, LANES), jnp.float32)
        for b in range(blocks):
            hit = wanted == lane + float(b * LANES)
            onehot[here, b * LANES : (b + 1) * LANES] = jnp.where(hit, 1.0, 0.0).astype(jnp.bfloat16)
            lit = lit + jnp.where(hit, light[b : b + 1, :], 0.0)
        insol[here, :] = jnp.broadcast_to(jnp.sum(lit, axis=1, keepdims=True), (LANES, LANES))

    def put(at, s):
        back[at * LANES : (at + 1) * LANES, s * LANES : (s + 1) * LANES] = jnp.where(
            slots[s : s + 1, :] == column + float(at * LANES), 1.0, 0.0
        ).astype(jnp.bfloat16)

    for at in range(inside):
        pick(0, at)
    loads[3].wait()
    copies = []
    own = None
    arriving = pl.ds(pl.multiple_of(me * piece, piece), piece)
    for k in range(PARTS):
        part = part_of(k)
        here = pl.ds(pl.multiple_of(part * part_rows, part_rows), part_rows)
        for n in range(0, columns.shape[1], WIDE):
            gathered[k % 2, :, n : n + WIDE] = jnp.dot(
                onehot[here, :], columns[:, n : n + WIDE], preferred_element_type=jnp.float32
            ).astype(jnp.bfloat16)
        jobs = [
            functools.partial(put, at, s)
            for at in range(k * inside, (k + 1) * inside)
            for s in range(blocks)
        ]
        if k + 1 < PARTS:
            jobs += [functools.partial(pick, k + 1, at) for at in range(inside)]
        tiles = hidden // WIDE
        share = -(-len(jobs) // (2 * tiles))
        if k == 0:
            loads[4].wait()
        for n in range(0, hidden, WIDE):
            layer_one[k % 2, :, n : n + WIDE] = silu(
                jnp.dot(gathered[k % 2], w_in[:, n : n + WIDE], preferred_element_type=jnp.float32)
            ).astype(jnp.bfloat16)
            for job in jobs[:share]:
                job()
            jobs = jobs[share:]
        if k == 0:
            loads[5].wait()
        for n in range(0, hidden, WIDE):
            layer_two[k % 2, :, n : n + WIDE] = silu(
                jnp.dot(layer_one[k % 2], w_mid[:, n : n + WIDE], preferred_element_type=jnp.float32)
            ).astype(jnp.bfloat16)
            for job in jobs[:share]:
                job()
            jobs = jobs[share:]
        if k == 0:
            loads[6].wait()
        out = jnp.dot(layer_two[k % 2], w_out[...], preferred_element_type=jnp.float32)
        leaving[here, :] = (insol[here, :] * softplus(out[:, levels:])).astype(jnp.bfloat16)
        heat[here, :] = (insol[here, :] * out[:, :levels]).astype(jnp.bfloat16)
        if k == 0:
            pl.semaphore_wait(barrier, groups - 1)
        for j in range(per):
            to = part * per + lax.rem(my_place + j, per)
            source = leaving.at[pl.ds(pl.multiple_of(to * piece, piece), piece), :]
            if k == PARTS - 1 and j == 0:
                own = pltpu.make_async_copy(source, flux_ref.at[arriving, :], own_sem)
                own.start()
                continue
            copy = pltpu.make_async_remote_copy(
                src_ref=source,
                dst_ref=flux_ref.at[arriving, :],
                send_sem=send_sem.at[k * per + j],
                recv_sem=recv_sem.at[k * per + j],
                device_id={"grp": to},
                device_id_type=MESH,
            )
            copy.start()
            copies.append(copy)
    for at in range(rows // ROWS):
        here = pl.ds(at * ROWS, ROWS)
        heat_ref[here, :] = jnp.dot(
            back[here, :], heat[...], preferred_element_type=jnp.float32
        ).astype(jnp.bfloat16)
    own.wait()
    for copy in copies:
        copy.wait_recv()
    for copy in copies:
        copy.wait_send()


def finish(heat, flux, heat_hbm, flux_hbm, wide, sem):
    copies = [pltpu.make_async_copy(heat, heat_hbm, sem.at[FINISH])]
    copies[0].start()
    step = flux.shape[0] // FINISH
    for at in range(FINISH):
        here = pl.ds(at * step, step)
        wide[here, :] = flux[here, :].astype(jnp.float32)
        copy = pltpu.make_async_copy(wide.at[here, :], flux_hbm.at[here, :], sem.at[at])
        copy.start()
        copies.append(copy)
    for copy in copies:
        copy.wait()


def body(columns, cos_zenith, sunlit, span_map, w_in, w_mid, w_out):
    rows, feat = columns.shape
    groups = lax.axis_size("grp")
    hidden, width = w_out.shape
    levels = width // 2
    tiles = rows // LANES
    anywhere = pl.BlockSpec(memory_space=pl.ANY)
    bf16 = jnp.bfloat16
    heating, flux = pl.pallas_call(
        functools.partial(kernel, groups),
        out_shape=(
            pltpu.VMEM((rows, levels), bf16),
            pltpu.VMEM((rows, levels), bf16),
        ),
        in_specs=[anywhere] * 7,
        out_specs=(pl.BlockSpec(memory_space=pltpu.VMEM),) * 2,
        scratch_shapes=[
            pltpu.VMEM((rows, feat), bf16),
            pltpu.VMEM((tiles, LANES), bf16),
            pltpu.VMEM((tiles, LANES), jnp.int32),
            pltpu.VMEM((tiles, LANES), jnp.int32),
            pltpu.VMEM((feat, hidden), bf16),
            pltpu.VMEM((hidden, hidden), bf16),
            pltpu.VMEM((hidden, width), bf16),
            pltpu.VMEM((rows, rows), bf16),
            pltpu.VMEM((rows, rows), bf16),
            pltpu.VMEM((rows, LANES), jnp.float32),
            pltpu.VMEM((2, rows // PARTS, feat), bf16),
            pltpu.VMEM((2, rows // PARTS, hidden), bf16),
            pltpu.VMEM((2, rows // PARTS, hidden), bf16),
            pltpu.VMEM((rows, levels), bf16),
            pltpu.VMEM((rows, levels), bf16),
            pltpu.SemaphoreType.DMA((7,)),
            pltpu.SemaphoreType.DMA,
            pltpu.SemaphoreType.DMA((groups,)),
            pltpu.SemaphoreType.DMA((groups,)),
        ],
        compiler_params=pltpu.CompilerParams(
            collective_id=0, has_side_effects=True, vmem_limit_bytes=62 * 1024 * 1024
        ),
        cost_estimate=pl.CostEstimate(
            flops=2 * rows * (feat * hidden + hidden * hidden + hidden * width),
            bytes_accessed=6 * 1024 * 1024,
            transcendentals=2 * rows * hidden,
        ),
    )(
        columns,
        cos_zenith.reshape(tiles, LANES),
        sunlit.reshape(tiles, LANES),
        span_map.reshape(tiles, LANES),
        w_in,
        w_mid,
        w_out,
    )
    return pl.pallas_call(
        finish,
        out_shape=(
            jax.ShapeDtypeStruct((rows, levels), bf16),
            jax.ShapeDtypeStruct((rows, levels), jnp.float32),
        ),
        in_specs=[pl.BlockSpec(memory_space=pltpu.VMEM)] * 2,
        out_specs=(anywhere, anywhere),
        scratch_shapes=[
            pltpu.VMEM((rows, levels), jnp.float32),
            pltpu.SemaphoreType.DMA((FINISH + 1,)),
        ],
        compiler_params=pltpu.CompilerParams(vmem_limit_bytes=4 * 1024 * 1024),
    )(heating, flux)


def solution(mesh):
    in_specs = (
        P(("lon", "grp"), None),
        P(("lon", "grp")),
        P(("lon", "grp")),
        P(("lon", "grp")),
        P(),
        P(),
        P(),
    )
    out_specs = (P(("lon", "grp"), None), P(("lon", "grp"), None))
    return jax.shard_map(body, mesh=mesh, in_specs=in_specs, out_specs=out_specs, check_vma=False)
```
